32 devices in a mesh: energy: 8 (over z, x), section: 4 (over y, core).
Axes of the slice: x: 2, y: 2, z: 4, core: 2. Of those that a mesh axis runs over, the one named last changes fastest.
Arguments:
- propagator: bfloat16 [8, 4, 2, 384, 384], P('energy', 'section')
- forward_source: bfloat16 [8, 4, 384, 128], P('energy', 'section'), may hold values from -6 to 6
- backward_source: bfloat16 [8, 4, 384, 128], P('energy', 'section'), may hold values from -6 to 6
- left_orbital: int32 [32768], P('section'), may hold values from 0 to 1535, as said below
- right_orbital: int32 [32768], P('section'), may hold values from 0 to 1535
- phonon_shift: int32 [8], replicated, may hold values from -6 to 6
- coupling: float32 [8, 32768], P(None, 'section'), may hold values from 0.1 to 1
Outputs:
- self_energy: float32 [2, 8, 32768], P(None, 'energy', 'section')
The draws below stay inside these ranges and needn't reach their ends.
Inputs may be any that keep to these rules, and one draw needn't show every extreme that they name: left_orbital[p] and right_orbital[p] are orbitals of section p // 8192: both lie from (p // 8192) * 384 to that plus 1 * 384 - 1, and they differ by at most 24.
All inputs are finite; a program needn't handle non-finite values.
Results may differ from the reference program's by a relative error of at most 0.022.
Values may be sent and summed in bfloat16 or wider, within the bound.
A program may use at most 64 MiB of HBM per device.

```python
import math
import jax
import jax.numpy as jnp
from jax import lax

ORB = 384
RHS = 64
PHON = 8
SLAB_DEV = 1
NPAIR_DEV = 8192
ENERGIES = 8
SLABS = 4
NPAIRS = 32768
N_SECTION = 4


def draw_propagator(key, part):
    key_mag, key_angle, key_rand = jax.random.split(key, 3)
    diag_shape = (ENERGIES, SLABS, ORB)
    magnitude = jnp.exp(jax.random.uniform(key_mag, diag_shape, jnp.float32, math.log(0.55), math.log(0.9)))
    angle_draw = jax.random.uniform(key_angle, diag_shape, jnp.float32, -math.pi, math.pi)
    noise_scale = 0.18 / math.sqrt(2.0 * ORB)
    full_shape = (ENERGIES, SLABS, 2, ORB, ORB)
    random_part = jax.random.normal(key_rand, full_shape, jnp.float32) * noise_scale
    diagonal = jnp.stack([magnitude * jnp.cos(angle_draw), magnitude * jnp.sin(angle_draw)], axis=2)
    unit_matrix = jnp.eye(ORB, dtype=jnp.float32)
    return (random_part + diagonal[..., None] * unit_matrix).astype(jnp.bfloat16)


def pair_draw(key):
    inner = jax.random.fold_in(key, 7)
    key_left, key_step = jax.random.split(inner)
    span = SLAB_DEV * ORB
    position = jnp.arange(NPAIRS, dtype=jnp.int32)
    section = position // NPAIR_DEV
    within = position % NPAIR_DEV
    first = jax.random.randint(key_left, (NPAIRS,), 0, span, dtype=jnp.int32)
    offset_step = jax.random.randint(key_step, (NPAIRS,), -24, 25, dtype=jnp.int32)
    second = jnp.clip(first + offset_step, 0, span - 1)
    first = jnp.where(within == 0, 0, first)
    second = jnp.where(within == 0, 0, second)
    first = jnp.where(within == NPAIR_DEV - 1, span - 1, first)
    second = jnp.where(within == NPAIR_DEV - 1, span - 1, second)
    section_base = section * span
    return (first + section_base, second + section_base)


def draw_left_orbital(key, part):
    return pair_draw(key)[0]


def draw_right_orbital(key, part):
    return pair_draw(key)[1]


def with_ends(entries, key, least, high):
    longest = entries.shape.index(max(entries.shape))
    spots = []
    for shift in (0, 1):
        where = [jax.random.randint(jax.random.fold_in(key, axis), (), 0, length) for axis, length in enumerate(entries.shape)]
        where[longest] = (where[longest] + shift) % entries.shape[longest]
        spots.append(tuple(where))
    return entries.at[spots[0]].set(least).at[spots[1]].set(high)


def steps_of(own_key, dims, cuts, least, high):
    loudness, own = 1.0, jax.random.fold_in(own_key, 6)
    for axis_at, blocks in cuts:
        steps = jnp.exp(jax.random.uniform(jax.random.fold_in(own, axis_at), (blocks,), jnp.float32, least / len(cuts), high / len(cuts)))
        loudness = loudness * jnp.repeat(steps, dims[axis_at] // blocks).reshape([-1 if axis == axis_at else 1 for axis in range(len(dims))])
    return loudness


def centred(stream_key, extent, scale, reach, cuts=(), held_as=jnp.bfloat16):
    result = jax.random.normal(stream_key, extent, jnp.float32) * scale
    if len(cuts) > 0:
        result = steps_of(stream_key, extent, cuts, -0.22, 0.18) * result
    return jnp.clip(result, min=-reach, max=reach).astype(held_as)


def setup_inputs(seed: int = 0) -> dict:
    streams_of = jax.random.split(jax.random.key(seed), 8)
    return {
        "propagator": draw_propagator(jax.random.fold_in(streams_of[7], 71), 0),
        "forward_source": centred(streams_of[1], (ENERGIES, SLABS, ORB, 2 * RHS), 1.0, 6.0, ((0, 8), (1, 4))),
        "backward_source": centred(streams_of[2], (ENERGIES, SLABS, ORB, 2 * RHS), 1.0, 6.0, ((0, 8), (1, 4))),
        "left_orbital": draw_left_orbital(jax.random.fold_in(streams_of[7], 71), 0),
        "right_orbital": draw_right_orbital(jax.random.fold_in(streams_of[7], 71), 0),
        "phonon_shift": with_ends(jax.random.randint(streams_of[5], (PHON,), -6, 7), jax.random.fold_in(streams_of[5], 1), -6, 6).astype(jnp.int32),
        "coupling": jnp.clip(jnp.exp(math.log(1.0) - 2.3025851 * jax.random.uniform(streams_of[6], (PHON, NPAIRS), jnp.float32) ** steps_of(streams_of[6], (PHON, NPAIRS), ((1, 4),), -0.2, 0.2)), 0.1, 1.0),
    }


def complex_product(matrix, columns, adjoint):
    left_real = matrix.astype(jnp.float32)
    right_real = columns.astype(jnp.float32)
    half = right_real.shape[1] // 2
    if adjoint:
        product = jnp.einsum('cji,jn->cin', left_real, right_real, precision=lax.Precision.HIGHEST)
        real_part = product[0, :, :half] + product[1, :, half:]
        imag_part = product[0, :, half:] - product[1, :, :half]
    else:
        product = jnp.einsum('cij,jn->cin', left_real, right_real, precision=lax.Precision.HIGHEST)
        real_part = product[0, :, :half] - product[1, :, half:]
        imag_part = product[0, :, half:] + product[1, :, :half]
    return jnp.concatenate([real_part, imag_part], axis=1)


def as_pair(joined):
    width = joined.shape[0]
    return jnp.stack([joined[:, :width], joined[:, width:]])


def section_maps(blocks, forward_src, backward_src):
    count = blocks.shape[0]
    composite = jnp.concatenate([blocks[0, 0], blocks[0, 1]], axis=1)
    forward_part = forward_src[0]
    for j in range(1, count):
        composite = complex_product(blocks[j], composite, False).astype(jnp.bfloat16)
        forward_part = (complex_product(blocks[j], forward_part, False) + forward_src[j]).astype(jnp.bfloat16)
    backward_part = backward_src[count - 1]
    for j in range(count - 2, -1, -1):
        backward_part = (complex_product(blocks[j], backward_part, True) + backward_src[j]).astype(jnp.bfloat16)
    return composite, forward_part, backward_part


def forward_pass(blocks, sources, start_state):
    current = start_state
    results = []
    for j in range(blocks.shape[0]):
        current = (complex_product(blocks[j], current, False) + sources[j]).astype(jnp.bfloat16)
        results.append(current)
    return jnp.stack(results)


def backward_pass(blocks, sources, start_state):
    current = start_state
    results = [None] * blocks.shape[0]
    for j in range(blocks.shape[0] - 1, -1, -1):
        current = (complex_product(blocks[j], current, True) + sources[j]).astype(jnp.bfloat16)
        results[j] = current
    return jnp.stack(results)


def lesser(field_rows, adjoint_rows, left_index, right_index, modes):
    left_rows = jnp.take(field_rows, left_index, axis=0).astype(jnp.float32)
    right_rows = jnp.take(adjoint_rows, right_index, axis=0).astype(jnp.float32)
    real_part = jnp.sum(left_rows[:, :modes] * right_rows[:, :modes] + left_rows[:, modes:] * right_rows[:, modes:], axis=1)
    imag_part = jnp.sum(left_rows[:, modes:] * right_rows[:, :modes] - left_rows[:, :modes] * right_rows[:, modes:], axis=1)
    return jnp.stack([real_part, imag_part]) * (modes ** -0.5)


def shifted_sum(portion, begin_at, own_energy, phonon_shift, coupling):
    count = portion.shape[1]
    positions = begin_at + jnp.arange(count, dtype=jnp.int32)
    summed = jnp.zeros((portion.shape[0], own_energy.shape[0], portion.shape[2]), jnp.float32)
    for k in range(phonon_shift.shape[0]):
        selector = (positions[None, :] == (own_energy - phonon_shift[k])[:, None]).astype(jnp.float32)
        moved = jnp.einsum('ef,cfp->cep', selector, portion.astype(jnp.float32), precision=lax.Precision.HIGHEST)
        summed = summed + coupling[k][None, None, :] * moved
    return summed


def reference(propagator, forward_source, backward_source, left_orbital, right_orbital, phonon_shift, coupling):
    def per_energy(members):
        blocks_all, forward_all, backward_all = members
        blocks = blocks_all.reshape(N_SECTION, SLAB_DEV, 2, ORB, ORB)
        forward_src = forward_all.reshape(N_SECTION, SLAB_DEV, ORB, 2 * RHS)
        backward_src = backward_all.reshape(N_SECTION, SLAB_DEV, ORB, 2 * RHS)
        composite, forward_part, backward_part = jax.vmap(section_maps)(blocks, forward_src, backward_src)
        zero_state = jnp.zeros((ORB, 2 * RHS), jnp.bfloat16)

        def forward_step(current, parts):
            matrix, vector = parts
            following = (complex_product(as_pair(matrix), current, False) + vector).astype(jnp.bfloat16)
            return following, current

        def backward_step(current, parts):
            matrix, vector = parts
            following = (complex_product(as_pair(matrix), current, True) + vector).astype(jnp.bfloat16)
            return following, current

        final_fwd, incoming = lax.scan(forward_step, zero_state, (composite, forward_part))
        final_bwd, returning = lax.scan(backward_step, zero_state, (composite, backward_part), reverse=True)
        fields = jax.vmap(forward_pass)(blocks, forward_src, incoming)
        adjoints = jax.vmap(backward_pass)(blocks, backward_src, returning)
        return lesser(fields.reshape(-1, 2 * RHS), adjoints.reshape(-1, 2 * RHS), left_orbital, right_orbital, RHS)

    lesser_part = lax.map(per_energy, (propagator, forward_source, backward_source))
    lesser_part = jnp.transpose(lesser_part, (1, 0, 2))
    return shifted_sum(lesser_part, jnp.int32(0), jnp.arange(ENERGIES, dtype=jnp.int32), phonon_shift, coupling)
```

```python
import functools
import jax
import jax.numpy as jnp
from jax import lax
from jax.experimental import pallas as pl
from jax.experimental.pallas import tpu as pltpu
from jax.sharding import PartitionSpec as P

MESH = pl.DeviceIdType.MESH
F32 = jnp.float32
BF16 = jnp.bfloat16
LANES = 128
FOLD = 64
REACH = 6


def sweep_kernel(
    energies, sections,
    prop_hbm, fsrc_hbm, bsrc_hbm, left_hbm, right_hbm, shift_ref, coup_hbm,
    out_ref,
    prop, fsrc, bsrc, left, right, coup,
    bsrc_t, chosen, weight,
    y, w_t, y_in, w_in,
    table, parts, sent, held, totals, gathered,
    load_sems, fwd_send, fwd_recv, bwd_send, bwd_recv,
    send_one, recv_one, send_two, recv_two,
):
    me = lax.axis_index("energy")
    s = lax.axis_index("section")
    orb = prop.shape[1]
    cols = y.shape[1]
    half = cols // 2
    block = chosen.shape[2]
    rows = block // LANES

    barrier = pltpu.get_barrier_semaphore()
    for j in range(1, energies):
        pl.semaphore_signal(
            barrier, inc=1, device_id={"energy": lax.rem(me + j, energies)}, device_id_type=MESH
        )

    @pl.when(s > 0)
    def _():
        pl.semaphore_signal(barrier, inc=1, device_id={"section": s - 1}, device_id_type=MESH)

    @pl.when(s < sections - 1)
    def _():
        pl.semaphore_signal(barrier, inc=1, device_id={"section": s + 1}, device_id_type=MESH)

    own = pl.ds(pl.multiple_of(me * block, LANES), block)
    loads = [
        pltpu.make_async_copy(fsrc_hbm, fsrc, load_sems.at[0]),
        pltpu.make_async_copy(bsrc_hbm, bsrc, load_sems.at[1]),
        pltpu.make_async_copy(left_hbm, left, load_sems.at[2]),
        pltpu.make_async_copy(right_hbm, right, load_sems.at[3]),
        pltpu.make_async_copy(prop_hbm, prop, load_sems.at[4]),
        pltpu.make_async_copy(coup_hbm.at[:, own], coup, load_sems.at[5]),
    ]
    for load in loads:
        load.start()

    zeros = jnp.zeros((REACH,) + held.shape[1:], held.dtype)
    held[pl.ds(0, REACH)] = zeros
    held[pl.ds(REACH + energies, REACH)] = zeros

    fwd = pltpu.make_async_remote_copy(
        src_ref=y, dst_ref=y_in, send_sem=fwd_send, recv_sem=fwd_recv,
        device_id={"section": lax.rem(s + 1, sections)}, device_id_type=MESH,
    )
    bwd = pltpu.make_async_remote_copy(
        src_ref=w_t, dst_ref=w_in, send_sem=bwd_send, recv_sem=bwd_recv,
        device_id={"section": lax.rem(s + sections - 1, sections)}, device_id_type=MESH,
    )

    loads[1].wait()
    bsrc_t[...] = bsrc[...].astype(F32).T
    for at in (0, 2, 3, 4, 5):
        loads[at].wait()
    base = s * orb

    def choose(b, carry):
        spot = lax.broadcasted_iota(jnp.int32, (orb, LANES), 0)
        for i in range(rows):
            row = left[pl.ds(b * rows + i, 1), :] - base
            chosen[b, :, i * LANES:(i + 1) * LANES] = jnp.where(spot == row, 1.0, 0.0).astype(BF16)
        return carry

    greeted = (energies - 1) + (s > 0).astype(jnp.int32) + (s < sections - 1).astype(jnp.int32)
    pl.semaphore_wait(barrier, greeted)

    def turn(t, carry):
        @pl.when(s == t)
        def _():
            @pl.when(s == 0)
            def _():
                y[...] = fsrc[...]

            @pl.when(s > 0)
            def _():
                fwd.wait_recv()
                current = y_in[...]
                first = jnp.dot(prop[0], current, preferred_element_type=F32)
                second = jnp.dot(prop[1], current, preferred_element_type=F32)
                lane = lax.broadcasted_iota(jnp.int32, second.shape, 1)
                crossed = pltpu.roll(second, half, 1)
                crossed = jnp.where(lane < half, -crossed, crossed)
                y[...] = (first + crossed + fsrc[...].astype(F32)).astype(BF16)

            @pl.when(s < sections - 1)
            def _():
                fwd.start()

        @pl.when(s == sections - 1 - t)
        def _():
            @pl.when(s == sections - 1)
            def _():
                w_t[...] = bsrc_t[...].astype(BF16)

            @pl.when(s < sections - 1)
            def _():
                bwd.wait_recv()
                current = w_in[...]
                first = jnp.dot(current, prop[0], preferred_element_type=F32)
                second = jnp.dot(current, prop[1], preferred_element_type=F32)
                crossed = jnp.concatenate([second[half:], -second[:half]], axis=0)
                w_t[...] = (first + crossed + bsrc_t[...]).astype(BF16)

            @pl.when(s > 0)
            def _():
                bwd.start()

        @pl.when(t < sections - 1)
        def _():
            lax.fori_loop(
                t * energies // (sections - 1), (t + 1) * energies // (sections - 1), choose, 0
            )

        return carry

    lax.fori_loop(0, sections, turn, 0)

    scale = half ** (-0.5)
    ahead = y[...]
    wide = ahead.astype(F32)
    lane = lax.broadcasted_iota(jnp.int32, wide.shape, 1)
    turned = pltpu.roll(wide, half, 1)
    turned = jnp.where(lane < half, turned, -turned).astype(BF16)
    behind = w_t[...].astype(F32).T.astype(BF16)
    both = (((1,), (1,)), ((), ()))
    for member, operand in enumerate((ahead, turned)):
        product = lax.dot_general(behind, operand, both, preferred_element_type=F32)
        for tile in range(orb // LANES):
            folded = None
            for q in range(max(0, tile * 2 - 1), min(orb // FOLD, tile * 2 + 3)):
                piece = product[q * FOLD:(q + 1) * FOLD, tile * LANES:(tile + 1) * LANES]
                right_at = q * FOLD + lax.broadcasted_iota(jnp.int32, piece.shape, 0)
                left_at = tile * LANES + lax.broadcasted_iota(jnp.int32, piece.shape, 1)
                kept = jnp.where(jnp.abs(right_at - left_at) < FOLD // 2, piece, 0.0)
                folded = kept if folded is None else folded + kept
            table[member * FOLD:(member + 1) * FOLD, tile * LANES:(tile + 1) * LANES] = (
                folded * scale
            ).astype(BF16)

    def exchange_one(other):
        return pltpu.make_async_remote_copy(
            src_ref=sent.at[other], dst_ref=held.at[REACH + me],
            send_sem=send_one.at[other], recv_sem=recv_one.at[me],
            device_id={"energy": other}, device_id_type=MESH,
        )

    def exchange_two(other):
        return pltpu.make_async_remote_copy(
            src_ref=totals.at[other], dst_ref=gathered.at[me],
            send_sem=send_two.at[other], recv_sem=recv_two.at[me],
            device_id={"energy": other}, device_id_type=MESH,
        )

    def arrived(other, sems, buffer, at):
        return pltpu.make_async_remote_copy(
            src_ref=buffer.at[at], dst_ref=buffer.at[at],
            send_sem=sems.at[other], recv_sem=sems.at[other],
            device_id={"energy": other}, device_id_type=MESH,
        )

    def pick(b):
        spread = jnp.dot(table[...], chosen[b], preferred_element_type=F32)
        for i in range(rows):
            row = (right[pl.ds(b * rows + i, 1), :] - base) & (FOLD - 1)
            spot = lax.broadcasted_iota(jnp.int32, (FOLD, LANES), 0) == row
            for member in range(2):
                piece = spread[member * FOLD:(member + 1) * FOLD, i * LANES:(i + 1) * LANES]
                parts[pl.ds(member * rows + i, 1), :] = jnp.sum(
                    jnp.where(spot, piece, 0.0), axis=0, keepdims=True
                )
        return parts[...].astype(BF16)

    def serve(j, carry):
        other = lax.rem(me + j, energies)
        sent[other] = pick(other)
        exchange_one(other).start()
        return carry

    lax.fori_loop(1, energies, serve, 0)
    held[REACH + me] = pick(me)

    for k in range(coup.shape[0]):
        for i in range(rows):
            line = coup[k:k + 1, i * LANES:(i + 1) * LANES]
            weight[k, i:i + 1, :] = line
            weight[k, rows + i:rows + i + 1, :] = line

    def await_one(j, carry):
        other = lax.rem(me + j, energies)
        arrived(other, recv_one, held, REACH + other).wait_recv()
        return carry

    lax.fori_loop(1, energies, await_one, 0)

    total = None
    for k in range(coup.shape[0]):
        moved = held[pl.ds(REACH - shift_ref[k], energies)].astype(F32)
        term = weight[k][None] * moved
        total = term if total is None else total + term
    totals[...] = total.astype(BF16)

    def send_back(j, carry):
        exchange_two(lax.rem(me + j, energies)).start()
        return carry

    lax.fori_loop(1, energies, send_back, 0)
    gathered[me] = totals[me]

    def await_two(j, carry):
        other = lax.rem(me + j, energies)
        arrived(other, recv_two, gathered, other).wait_recv()
        return carry

    lax.fori_loop(1, energies, await_two, 0)
    for b in range(energies):
        for member in range(2):
            out_ref[member, b * rows:(b + 1) * rows, :] = gathered[
                b, member * rows:(member + 1) * rows, :
            ].astype(F32)

    def settle(j, carry):
        other = lax.rem(me + j, energies)
        exchange_one(other).wait_send()
        exchange_two(other).wait_send()
        return carry

    lax.fori_loop(1, energies, settle, 0)

    @pl.when(s < sections - 1)
    def _():
        fwd.wait_send()

    @pl.when(s > 0)
    def _():
        bwd.wait_send()


def on_device(
    propagator, forward_source, backward_source, left_orbital, right_orbital, phonon_shift, coupling
):
    energies = lax.axis_size("energy")
    sections = lax.axis_size("section")
    orb = propagator.shape[3]
    cols = forward_source.shape[3]
    pairs = left_orbital.shape[0]
    phonons = coupling.shape[0]
    block = pairs // energies
    rows = block // LANES
    tall = max(16, 2 * rows)
    anywhere = pl.BlockSpec(memory_space=pl.ANY)
    out = pl.pallas_call(
        functools.partial(sweep_kernel, energies, sections),
        out_shape=jax.ShapeDtypeStruct((2, pairs // LANES, LANES), F32),
        in_specs=[anywhere] * 5 + [pl.BlockSpec(memory_space=pltpu.SMEM), anywhere],
        out_specs=pl.BlockSpec(memory_space=pltpu.VMEM),
        scratch_shapes=[
            pltpu.VMEM((2, orb, orb), BF16),
            pltpu.VMEM((orb, cols), BF16),
            pltpu.VMEM((orb, cols), BF16),
            pltpu.VMEM((pairs // LANES, LANES), jnp.int32),
            pltpu.VMEM((pairs // LANES, LANES), jnp.int32),
            pltpu.VMEM((phonons, block), F32),
            pltpu.VMEM((cols, orb), F32),
            pltpu.VMEM((energies, orb, block), BF16),
            pltpu.VMEM((phonons, tall, LANES), F32),
            pltpu.VMEM((orb, cols), BF16),
            pltpu.VMEM((cols, orb), BF16),
            pltpu.VMEM((orb, cols), BF16),
            pltpu.VMEM((cols, orb), BF16),
            pltpu.VMEM((2 * FOLD, orb), BF16),
            pltpu.VMEM((tall, LANES), F32),
            pltpu.VMEM((energies, tall, LANES), BF16),
            pltpu.VMEM((energies + 2 * REACH, tall, LANES), BF16),
            pltpu.VMEM((energies, tall, LANES), BF16),
            pltpu.VMEM((energies, tall, LANES), BF16),
            pltpu.SemaphoreType.DMA((6,)),
            pltpu.SemaphoreType.DMA,
            pltpu.SemaphoreType.DMA,
            pltpu.SemaphoreType.DMA,
            pltpu.SemaphoreType.DMA,
            pltpu.SemaphoreType.DMA((energies,)),
            pltpu.SemaphoreType.DMA((energies,)),
            pltpu.SemaphoreType.DMA((energies,)),
            pltpu.SemaphoreType.DMA((energies,)),
        ],
        compiler_params=pltpu.CompilerParams(
            collective_id=0, has_side_effects=True, vmem_limit_bytes=40 * 2**20
        ),
    )(
        propagator.reshape(2, orb, orb),
        forward_source.reshape(orb, cols),
        backward_source.reshape(orb, cols),
        left_orbital.reshape(pairs // LANES, LANES),
        right_orbital.reshape(pairs // LANES, LANES),
        phonon_shift,
        coupling,
    )
    return out.reshape(2, 1, pairs)


def solution(mesh):
    placed = (
        P("energy", "section", None, None, None),
        P("energy", "section", None, None),
        P("energy", "section", None, None),
        P("section"),
        P("section"),
        P(),
        P(None, "section"),
    )
    return jax.shard_map(
        on_device,
        mesh=mesh,
        in_specs=placed,
        out_specs=P(None, "energy", "section"),
        check_vma=False,
    )
```

```python
import functools
import jax
import jax.numpy as jnp
from jax import lax
from jax.experimental import pallas as pl
from jax.experimental.pallas import tpu as pltpu
from jax.sharding import PartitionSpec as P

MESH = pl.DeviceIdType.MESH
F32 = jnp.float32
BF16 = jnp.bfloat16
LANES = 128
FOLD = 64
REACH = 6


def sweep_kernel(
    energies, sections,
    prop_hbm, fsrc_hbm, bsrc_hbm, left_hbm, right_hbm, shift_ref, coup_hbm,
    out_ref,
    prop, fsrc, bsrc, left, right, coup,
    bsrc_t, chosen, weight,
    y, w_t, y_in, w_in, w_end,
    table, parts, sent, held, totals, gathered,
    load_sems, fwd_send, fwd_recv, bwd_send, bwd_recv, end_send, end_recv,
    send_one, recv_one, send_two, recv_two,
):
    me = lax.axis_index("energy")
    s = lax.axis_index("section")
    orb = prop.shape[1]
    cols = y.shape[1]
    half = cols // 2
    block = chosen.shape[2]
    rows = block // LANES

    barrier = pltpu.get_barrier_semaphore()
    for j in range(1, energies):
        pl.semaphore_signal(
            barrier, inc=1, device_id={"energy": lax.rem(me + j, energies)}, device_id_type=MESH
        )

    @pl.when(s > 0)
    def _():
        pl.semaphore_signal(barrier, inc=1, device_id={"section": s - 1}, device_id_type=MESH)

    @pl.when(s < sections - 1)
    def _():
        pl.semaphore_signal(barrier, inc=1, device_id={"section": s + 1}, device_id_type=MESH)

    own = pl.ds(pl.multiple_of(me * block, LANES), block)
    loads = [
        pltpu.make_async_copy(fsrc_hbm, fsrc, load_sems.at[0]),
        pltpu.make_async_copy(bsrc_hbm, bsrc, load_sems.at[1]),
        pltpu.make_async_copy(left_hbm, left, load_sems.at[2]),
        pltpu.make_async_copy(right_hbm, right, load_sems.at[3]),
        pltpu.make_async_copy(prop_hbm, prop, load_sems.at[4]),
        pltpu.make_async_copy(coup_hbm.at[:, own], coup, load_sems.at[5]),
    ]
    for load in loads:
        load.start()

    zeros = jnp.zeros((REACH,) + held.shape[1:], held.dtype)
    held[pl.ds(0, REACH)] = zeros
    held[pl.ds(REACH + energies, REACH)] = zeros

    after, before = lax.rem(s + 1, sections), lax.rem(s + sections - 1, sections)

    def passed(source, target, send_sem, recv_sem, to):
        return pltpu.make_async_remote_copy(
            src_ref=source, dst_ref=target, send_sem=send_sem, recv_sem=recv_sem,
            device_id={"section": to}, device_id_type=MESH,
        )

    fwd_first = passed(fsrc_hbm, y_in, fwd_send, fwd_recv, after)
    fwd = passed(y, y_in, fwd_send, fwd_recv, after)
    bwd_first = passed(bsrc_hbm, w_end, end_send, end_recv, before)
    bwd = passed(w_t, w_in, bwd_send, bwd_recv, before)
    base = s * orb

    def choose(b, carry):
        spot = lax.broadcasted_iota(jnp.int32, (orb, LANES), 0)
        for i in range(rows):
            row = left[pl.ds(b * rows + i, 1), :] - base
            chosen[b, :, i * LANES:(i + 1) * LANES] = jnp.where(spot == row, 1.0, 0.0).astype(BF16)
        return carry

    greeted = (energies - 1) + (s > 0).astype(jnp.int32) + (s < sections - 1).astype(jnp.int32)
    pl.semaphore_wait(barrier, greeted)

    @pl.when(s == 0)
    def _():
        fwd_first.start()

    @pl.when(s == sections - 1)
    def _():
        bwd_first.start()

    for at in (0, 1, 2):
        loads[at].wait()
    bsrc_t[...] = bsrc[...].astype(F32).T

    @pl.when(s == 0)
    def _():
        y[...] = fsrc[...]

    @pl.when(s == sections - 1)
    def _():
        w_t[...] = bsrc_t[...].astype(BF16)

    def build(t):
        lax.fori_loop(
            t * energies // (sections - 1), (t + 1) * energies // (sections - 1), choose, 0
        )

    build(0)
    loads[4].wait()

    def turn(t, carry):
        @pl.when(s == t)
        def _():
            fwd.wait_recv()
            current = y_in[...]
            first = jnp.dot(prop[0], current, preferred_element_type=F32)
            second = jnp.dot(prop[1], current, preferred_element_type=F32)
            lane = lax.broadcasted_iota(jnp.int32, second.shape, 1)
            crossed = pltpu.roll(second, half, 1)
            crossed = jnp.where(lane < half, -crossed, crossed)
            y[...] = (first + crossed + fsrc[...].astype(F32)).astype(BF16)

            @pl.when(s < sections - 1)
            def _():
                fwd.start()

        @pl.when(s == sections - 1 - t)
        def _():
            @pl.when(t == 1)
            def _():
                bwd_first.wait_recv()
                w_in[...] = w_end[...].astype(F32).T.astype(BF16)

            @pl.when(t > 1)
            def _():
                bwd.wait_recv()

            current = w_in[...]
            first = jnp.dot(current, prop[0], preferred_element_type=F32)
            second = jnp.dot(current, prop[1], preferred_element_type=F32)
            crossed = jnp.concatenate([second[half:], -second[:half]], axis=0)
            w_t[...] = (first + crossed + bsrc_t[...]).astype(BF16)

            @pl.when(s > 0)
            def _():
                bwd.start()

        @pl.when(t < sections - 1)
        def _():
            build(t)

        return carry

    lax.fori_loop(1, sections, turn, 0)
    loads[3].wait()
    loads[5].wait()

    for k in range(coup.shape[0]):
        for i in range(rows):
            line = coup[k:k + 1, i * LANES:(i + 1) * LANES]
            weight[k, i:i + 1, :] = line
            weight[k, rows + i:rows + i + 1, :] = line

    scale = half ** (-0.5)
    ahead = y[...]
    wide = ahead.astype(F32)
    lane = lax.broadcasted_iota(jnp.int32, wide.shape, 1)
    turned = pltpu.roll(wide, half, 1)
    turned = jnp.where(lane < half, turned, -turned).astype(BF16)
    behind = w_t[...].astype(F32).T.astype(BF16)
    both = (((1,), (1,)), ((), ()))
    for member, operand in enumerate((ahead, turned)):
        product = lax.dot_general(behind, operand, both, preferred_element_type=F32)
        for tile in range(orb // LANES):
            folded = None
            for q in range(max(0, tile * 2 - 1), min(orb // FOLD, tile * 2 + 3)):
                piece = product[q * FOLD:(q + 1) * FOLD, tile * LANES:(tile + 1) * LANES]
                right_at = q * FOLD + lax.broadcasted_iota(jnp.int32, piece.shape, 0)
                left_at = tile * LANES + lax.broadcasted_iota(jnp.int32, piece.shape, 1)
                kept = jnp.where(jnp.abs(right_at - left_at) < FOLD // 2, piece, 0.0)
                folded = kept if folded is None else folded + kept
            table[member * FOLD:(member + 1) * FOLD, tile * LANES:(tile + 1) * LANES] = (
                folded * scale
            ).astype(BF16)

    def exchange_one(other):
        return pltpu.make_async_remote_copy(
            src_ref=sent.at[other], dst_ref=held.at[REACH + me],
            send_sem=send_one.at[other], recv_sem=recv_one.at[me],
            device_id={"energy": other}, device_id_type=MESH,
        )

    def exchange_two(other):
        return pltpu.make_async_remote_copy(
            src_ref=totals.at[other], dst_ref=gathered.at[me],
            send_sem=send_two.at[other], recv_sem=recv_two.at[me],
            device_id={"energy": other}, device_id_type=MESH,
        )

    def arrived(other, sems, buffer, at):
        return pltpu.make_async_remote_copy(
            src_ref=buffer.at[at], dst_ref=buffer.at[at],
            send_sem=sems.at[other], recv_sem=sems.at[other],
            device_id={"energy": other}, device_id_type=MESH,
        )

    def pick(b):
        spread = jnp.dot(table[...], chosen[b], preferred_element_type=F32)
        for i in range(rows):
            row = (right[pl.ds(b * rows + i, 1), :] - base) & (FOLD - 1)
            spot = lax.broadcasted_iota(jnp.int32, (FOLD, LANES), 0) == row
            for member in range(2):
                piece = spread[member * FOLD:(member + 1) * FOLD, i * LANES:(i + 1) * LANES]
                parts[pl.ds(member * rows + i, 1), :] = jnp.sum(
                    jnp.where(spot, piece, 0.0), axis=0, keepdims=True
                )
        return parts[...].astype(BF16)

    def serve(j, carry):
        other = lax.rem(me + j, energies)
        sent[other] = pick(other)
        exchange_one(other).start()
        return carry

    lax.fori_loop(1, energies, serve, 0)
    held[REACH + me] = pick(me)

    def await_one(j, carry):
        other = lax.rem(me + j, energies)
        arrived(other, recv_one, held, REACH + other).wait_recv()
        return carry

    lax.fori_loop(1, energies, await_one, 0)

    total = None
    for k in range(coup.shape[0]):
        moved = held[pl.ds(REACH - shift_ref[k], energies)].astype(F32)
        term = weight[k][None] * moved
        total = term if total is None else total + term
    totals[...] = total.astype(BF16)

    def send_back(j, carry):
        exchange_two(lax.rem(me + j, energies)).start()
        return carry

    lax.fori_loop(1, energies, send_back, 0)
    gathered[me] = totals[me]

    def await_two(j, carry):
        other = lax.rem(me + j, energies)
        arrived(other, recv_two, gathered, other).wait_recv()
        return carry

    lax.fori_loop(1, energies, await_two, 0)
    for b in range(energies):
        for member in range(2):
            out_ref[member, b * rows:(b + 1) * rows, :] = gathered[
                b, member * rows:(member + 1) * rows, :
            ].astype(F32)

    def settle(j, carry):
        other = lax.rem(me + j, energies)
        exchange_one(other).wait_send()
        exchange_two(other).wait_send()
        return carry

    lax.fori_loop(1, energies, settle, 0)

    @pl.when(s < sections - 1)
    def _():
        fwd.wait_send()

    @pl.when(s == sections - 1)
    def _():
        bwd_first.wait_send()

    @pl.when((s > 0) & (s < sections - 1))
    def _():
        bwd.wait_send()


def on_device(
    propagator, forward_source, backward_source, left_orbital, right_orbital, phonon_shift, coupling
):
    energies = lax.axis_size("energy")
    sections = lax.axis_size("section")
    orb = propagator.shape[3]
    cols = forward_source.shape[3]
    pairs = left_orbital.shape[0]
    phonons = coupling.shape[0]
    block = pairs // energies
    rows = block // LANES
    tall = max(16, 2 * rows)
    in_hbm = pl.BlockSpec(memory_space=pltpu.HBM)
    out = pl.pallas_call(
        functools.partial(sweep_kernel, energies, sections),
        out_shape=jax.ShapeDtypeStruct((2, pairs // LANES, LANES), F32),
        in_specs=[in_hbm] * 5 + [pl.BlockSpec(memory_space=pltpu.SMEM), in_hbm],
        out_specs=pl.BlockSpec(memory_space=pltpu.VMEM),
        scratch_shapes=[
            pltpu.VMEM((2, orb, orb), BF16),
            pltpu.VMEM((orb, cols), BF16),
            pltpu.VMEM((orb, cols), BF16),
            pltpu.VMEM((pairs // LANES, LANES), jnp.int32),
            pltpu.VMEM((pairs // LANES, LANES), jnp.int32),
            pltpu.VMEM((phonons, block), F32),
            pltpu.VMEM((cols, orb), F32),
            pltpu.VMEM((energies, orb, block), BF16),
            pltpu.VMEM((phonons, tall, LANES), F32),
            pltpu.VMEM((orb, cols), BF16),
            pltpu.VMEM((cols, orb), BF16),
            pltpu.VMEM((orb, cols), BF16),
            pltpu.VMEM((cols, orb), BF16),
            pltpu.VMEM((orb, cols), BF16),
            pltpu.VMEM((2 * FOLD, orb), BF16),
            pltpu.VMEM((tall, LANES), F32),
            pltpu.VMEM((energies, tall, LANES), BF16),
            pltpu.VMEM((energies + 2 * REACH, tall, LANES), BF16),
            pltpu.VMEM((energies, tall, LANES), BF16),
            pltpu.VMEM((energies, tall, LANES), BF16),
            pltpu.SemaphoreType.DMA((6,)),
            pltpu.SemaphoreType.DMA,
            pltpu.SemaphoreType.DMA,
            pltpu.SemaphoreType.DMA,
            pltpu.SemaphoreType.DMA,
            pltpu.SemaphoreType.DMA,
            pltpu.SemaphoreType.DMA,
            pltpu.SemaphoreType.DMA((energies,)),
            pltpu.SemaphoreType.DMA((energies,)),
            pltpu.SemaphoreType.DMA((energies,)),
            pltpu.SemaphoreType.DMA((energies,)),
        ],
        compiler_params=pltpu.CompilerParams(
            collective_id=0, has_side_effects=True, vmem_limit_bytes=63 * 2**20
        ),
    )(
        propagator.reshape(2, orb, orb),
        forward_source.reshape(orb, cols),
        backward_source.reshape(orb, cols),
        left_orbital.reshape(pairs // LANES, LANES),
        right_orbital.reshape(pairs // LANES, LANES),
        phonon_shift,
        coupling,
    )
    return out.reshape(2, 1, pairs)


def solution(mesh):
    placed = (
        P("energy", "section", None, None, None),
        P("energy", "section", None, None),
        P("energy", "section", None, None),
        P("section"),
        P("section"),
        P(),
        P(None, "section"),
    )
    return jax.shard_map(
        on_device,
        mesh=mesh,
        in_specs=placed,
        out_specs=P(None, "energy", "section"),
        check_vma=False,
    )
```

```python
import functools
import jax
import jax.numpy as jnp
from jax import lax
from jax.experimental import pallas as pl
from jax.experimental.pallas import tpu as pltpu
from jax.sharding import PartitionSpec as P

MESH = pl.DeviceIdType.MESH
F32 = jnp.float32
BF16 = jnp.bfloat16
LANES = 128
DEEP = 256
DEEP_BITS = 8
FOLD = 64
REACH = 6


def sweep_kernel(
    energies, sections,
    prop_hbm, fsrc_hbm, bsrc_hbm, left_hbm, right_hbm, shift_ref, coup_hbm,
    out_ref,
    prop, fsrc, bsrc, left, right, coup,
    bsrc_t, chosen, weight,
    y, w_t, y_in, w_in, w_end,
    table, parts, sent, held, totals, gathered,
    load_sems, fwd_send, fwd_recv, bwd_send, bwd_recv, end_send, end_recv,
    send_one, recv_one, send_two, recv_two,
):
    me = lax.axis_index("energy")
    s = lax.axis_index("section")
    orb = prop.shape[1]
    cols = y.shape[1]
    half = cols // 2
    block = chosen.shape[2]
    rows = block // LANES
    groups = table.shape[0] // (2 * FOLD)

    barrier = pltpu.get_barrier_semaphore()
    for j in range(1, energies):
        pl.semaphore_signal(
            barrier, inc=1, device_id={"energy": lax.rem(me + j, energies)}, device_id_type=MESH
        )

    @pl.when(s > 0)
    def _():
        pl.semaphore_signal(barrier, inc=1, device_id={"section": s - 1}, device_id_type=MESH)

    @pl.when(s < sections - 1)
    def _():
        pl.semaphore_signal(barrier, inc=1, device_id={"section": s + 1}, device_id_type=MESH)

    own = pl.ds(pl.multiple_of(me * block, LANES), block)
    loads = [
        pltpu.make_async_copy(fsrc_hbm, fsrc, load_sems.at[0]),
        pltpu.make_async_copy(bsrc_hbm, bsrc, load_sems.at[1]),
        pltpu.make_async_copy(left_hbm, left, load_sems.at[2]),
        pltpu.make_async_copy(right_hbm, right, load_sems.at[3]),
        pltpu.make_async_copy(prop_hbm, prop, load_sems.at[4]),
        pltpu.make_async_copy(coup_hbm.at[:, own], coup, load_sems.at[5]),
    ]
    for load in loads:
        load.start()

    table[...] = jnp.zeros(table.shape, table.dtype)
    zeros = jnp.zeros((REACH,) + held.shape[1:], held.dtype)
    held[pl.ds(0, REACH)] = zeros
    held[pl.ds(REACH + energies, REACH)] = zeros

    after, before = lax.rem(s + 1, sections), lax.rem(s + sections - 1, sections)

    def passed(source, target, send_sem, recv_sem, to):
        return pltpu.make_async_remote_copy(
            src_ref=source, dst_ref=target, send_sem=send_sem, recv_sem=recv_sem,
            device_id={"section": to}, device_id_type=MESH,
        )

    fwd_first = passed(fsrc_hbm, y_in, fwd_send, fwd_recv, after)
    fwd = passed(y, y_in, fwd_send, fwd_recv, after)
    bwd_first = passed(bsrc_hbm, w_end, end_send, end_recv, before)
    bwd = passed(w_t, w_in, bwd_send, bwd_recv, before)
    base = s * orb

    def choose(b, carry):
        spot = lax.broadcasted_iota(jnp.int32, (DEEP, LANES), 0)
        for i in range(rows):
            row = (left[pl.ds(b * rows + i, 1), :] - base) & (DEEP - 1)
            chosen[b, :, i * LANES:(i + 1) * LANES] = jnp.where(spot == row, 1.0, 0.0).astype(BF16)
        return carry

    greeted = (energies - 1) + (s > 0).astype(jnp.int32) + (s < sections - 1).astype(jnp.int32)
    pl.semaphore_wait(barrier, greeted)

    @pl.when(s == 0)
    def _():
        fwd_first.start()

    @pl.when(s == sections - 1)
    def _():
        bwd_first.start()

    for at in (0, 1, 2):
        loads[at].wait()
    bsrc_t[...] = bsrc[...].astype(F32).T

    @pl.when(s == 0)
    def _():
        y[...] = fsrc[...]

    @pl.when(s == sections - 1)
    def _():
        w_t[...] = bsrc_t[...].astype(BF16)

    def build(t):
        lax.fori_loop(
            t * energies // (sections - 1), (t + 1) * energies // (sections - 1), choose, 0
        )

    build(0)
    loads[4].wait()

    def turn(t, carry):
        @pl.when(s == t)
        def _():
            fwd.wait_recv()
            current = y_in[...]
            first = jnp.dot(prop[0], current, preferred_element_type=F32)
            second = jnp.dot(prop[1], current, preferred_element_type=F32)
            lane = lax.broadcasted_iota(jnp.int32, second.shape, 1)
            crossed = pltpu.roll(second, half, 1)
            crossed = jnp.where(lane < half, -crossed, crossed)
            y[...] = (first + crossed + fsrc[...].astype(F32)).astype(BF16)

            @pl.when(s < sections - 1)
            def _():
                fwd.start()

        @pl.when(s == sections - 1 - t)
        def _():
            @pl.when(t == 1)
            def _():
                bwd_first.wait_recv()
                w_in[...] = w_end[...].astype(F32).T.astype(BF16)

            @pl.when(t > 1)
            def _():
                bwd.wait_recv()

            current = w_in[...]
            first = jnp.dot(current, prop[0], preferred_element_type=F32)
            second = jnp.dot(current, prop[1], preferred_element_type=F32)
            crossed = jnp.concatenate([second[half:], -second[:half]], axis=0)
            w_t[...] = (first + crossed + bsrc_t[...]).astype(BF16)

            @pl.when(s > 0)
            def _():
                bwd.start()

        @pl.when(t < sections - 1)
        def _():
            build(t)

        return carry

    lax.fori_loop(1, sections, turn, 0)
    loads[3].wait()
    loads[5].wait()

    for k in range(coup.shape[0]):
        for i in range(rows):
            line = coup[k:k + 1, i * LANES:(i + 1) * LANES]
            weight[k, i:i + 1, :] = line
            weight[k, rows + i:rows + i + 1, :] = line

    scale = half ** (-0.5)
    ahead = y[...]
    wide = ahead.astype(F32)
    lane = lax.broadcasted_iota(jnp.int32, wide.shape, 1)
    turned = pltpu.roll(wide, half, 1)
    turned = jnp.where(lane < half, turned, -turned).astype(BF16)
    behind = w_t[...].astype(F32).T.astype(BF16)
    both = (((1,), (1,)), ((), ()))
    for member, operand in enumerate((ahead, turned)):
        product = lax.dot_general(behind, operand, both, preferred_element_type=F32)
        for tile in range(orb // LANES):
            folded = None
            for q in range(max(0, tile * 2 - 1), min(orb // FOLD, tile * 2 + 3)):
                piece = product[q * FOLD:(q + 1) * FOLD, tile * LANES:(tile + 1) * LANES]
                right_at = q * FOLD + lax.broadcasted_iota(jnp.int32, piece.shape, 0)
                left_at = tile * LANES + lax.broadcasted_iota(jnp.int32, piece.shape, 1)
                kept = jnp.where(jnp.abs(right_at - left_at) < FOLD // 2, piece, 0.0)
                folded = kept if folded is None else folded + kept
            group, column = tile * LANES // DEEP, tile * LANES % DEEP
            top = (member * groups + group) * FOLD
            table[top:top + FOLD, column:column + LANES] = (folded * scale).astype(BF16)

    def exchange_one(other):
        return pltpu.make_async_remote_copy(
            src_ref=sent.at[other], dst_ref=held.at[REACH + me],
            send_sem=send_one.at[other], recv_sem=recv_one.at[me],
            device_id={"energy": other}, device_id_type=MESH,
        )

    def exchange_two(other):
        return pltpu.make_async_remote_copy(
            src_ref=totals.at[other], dst_ref=gathered.at[me],
            send_sem=send_two.at[other], recv_sem=recv_two.at[me],
            device_id={"energy": other}, device_id_type=MESH,
        )

    def arrived(other, sems, buffer, at):
        return pltpu.make_async_remote_copy(
            src_ref=buffer.at[at], dst_ref=buffer.at[at],
            send_sem=sems.at[other], recv_sem=sems.at[other],
            device_id={"energy": other}, device_id_type=MESH,
        )

    def product_of(b):
        return jnp.dot(table[...], chosen[b], preferred_element_type=F32)

    def pick(b, spread):
        eight = (8, LANES)
        for i in range(rows):
            right_at = (right[pl.ds(b * rows + i, 1), :] - base) & (FOLD - 1)
            group = lax.shift_right_logical(left[pl.ds(b * rows + i, 1), :] - base, DEEP_BITS)
            high = jnp.broadcast_to(
                group * (FOLD // 8) + lax.shift_right_logical(right_at, 3), eight
            )
            low = lax.broadcasted_iota(jnp.int32, eight, 0) == jnp.broadcast_to(right_at & 7, eight)
            for member in range(2):
                top = member * groups * FOLD
                pieces = [
                    spread[top + 8 * n:top + 8 * n + 8, i * LANES:(i + 1) * LANES]
                    for n in range(groups * FOLD // 8)
                ]
                width = 1 << (len(pieces) - 1).bit_length()
                while width > 1:
                    width //= 2
                    upper = (high & width) != 0
                    pieces = [
                        jnp.where(upper, pieces[n + width], piece)
                        if n + width < len(pieces) else piece
                        for n, piece in enumerate(pieces[:width])
                    ]
                parts[b, pl.ds(member * rows + i, 1), :] = jnp.sum(
                    jnp.where(low, pieces[0], 0.0), axis=0, keepdims=True
                )
        return parts[b].astype(BF16)

    if energies <= 8:
        spread = product_of(lax.rem(me + 1, energies))
        for j in range(1, energies + 1):
            other = lax.rem(me + j, energies)
            current = spread
            if j < energies:
                spread = product_of(lax.rem(me + j + 1, energies))
                sent[other] = pick(other, current)
                exchange_one(other).start()
            else:
                held[REACH + me] = pick(me, current)
    else:
        def serve(j, carry):
            other = lax.rem(me + j, energies)
            sent[other] = pick(other, product_of(other))
            exchange_one(other).start()
            return carry

        lax.fori_loop(1, energies, serve, 0)
        held[REACH + me] = pick(me, product_of(me))

    def await_one(j, carry):
        other = lax.rem(me + j, energies)
        arrived(other, recv_one, held, REACH + other).wait_recv()
        return carry

    lax.fori_loop(1, energies, await_one, 0)

    total = None
    for k in range(coup.shape[0]):
        moved = held[pl.ds(REACH - shift_ref[k], energies)].astype(F32)
        term = weight[k][None] * moved
        total = term if total is None else total + term
    totals[...] = total.astype(BF16)

    def send_back(j, carry):
        exchange_two(lax.rem(me + j, energies)).start()
        return carry

    lax.fori_loop(1, energies, send_back, 0)
    gathered[me] = totals[me]

    def await_two(j, carry):
        other = lax.rem(me + j, energies)
        arrived(other, recv_two, gathered, other).wait_recv()
        return carry

    lax.fori_loop(1, energies, await_two, 0)
    for b in range(energies):
        for member in range(2):
            out_ref[member, b * rows:(b + 1) * rows, :] = gathered[
                b, member * rows:(member + 1) * rows, :
            ].astype(F32)

    def settle(j, carry):
        other = lax.rem(me + j, energies)
        exchange_one(other).wait_send()
        exchange_two(other).wait_send()
        return carry

    lax.fori_loop(1, energies, settle, 0)

    @pl.when(s < sections - 1)
    def _():
        fwd.wait_send()

    @pl.when(s == sections - 1)
    def _():
        bwd_first.wait_send()

    @pl.when((s > 0) & (s < sections - 1))
    def _():
        bwd.wait_send()


def on_device(
    propagator, forward_source, backward_source, left_orbital, right_orbital, phonon_shift, coupling
):
    energies = lax.axis_size("energy")
    sections = lax.axis_size("section")
    orb = propagator.shape[3]
    cols = forward_source.shape[3]
    pairs = left_orbital.shape[0]
    phonons = coupling.shape[0]
    block = pairs // energies
    rows = block // LANES
    tall = max(16, 2 * rows)
    groups = pl.cdiv(orb, DEEP)
    in_hbm = pl.BlockSpec(memory_space=pltpu.HBM)
    out = pl.pallas_call(
        functools.partial(sweep_kernel, energies, sections),
        out_shape=jax.ShapeDtypeStruct((2, pairs // LANES, LANES), F32),
        in_specs=[in_hbm] * 5 + [pl.BlockSpec(memory_space=pltpu.SMEM), in_hbm],
        out_specs=pl.BlockSpec(memory_space=pltpu.VMEM),
        scratch_shapes=[
            pltpu.VMEM((2, orb, orb), BF16),
            pltpu.VMEM((orb, cols), BF16),
            pltpu.VMEM((orb, cols), BF16),
            pltpu.VMEM((pairs // LANES, LANES), jnp.int32),
            pltpu.VMEM((pairs // LANES, LANES), jnp.int32),
            pltpu.VMEM((phonons, block), F32),
            pltpu.VMEM((cols, orb), F32),
            pltpu.VMEM((energies, DEEP, block), BF16),
            pltpu.VMEM((phonons, tall, LANES), F32),
            pltpu.VMEM((orb, cols), BF16),
            pltpu.VMEM((cols, orb), BF16),
            pltpu.VMEM((orb, cols), BF16),
            pltpu.VMEM((cols, orb), BF16),
            pltpu.VMEM((orb, cols), BF16),
            pltpu.VMEM((2 * groups * FOLD, DEEP), BF16),
            pltpu.VMEM((energies, tall, LANES), F32),
            pltpu.VMEM((energies, tall, LANES), BF16),
            pltpu.VMEM((energies + 2 * REACH, tall, LANES), BF16),
            pltpu.VMEM((energies, tall, LANES), BF16),
            pltpu.VMEM((energies, tall, LANES), BF16),
            pltpu.SemaphoreType.DMA((6,)),
            pltpu.SemaphoreType.DMA,
            pltpu.SemaphoreType.DMA,
            pltpu.SemaphoreType.DMA,
            pltpu.SemaphoreType.DMA,
            pltpu.SemaphoreType.DMA,
            pltpu.SemaphoreType.DMA,
            pltpu.SemaphoreType.DMA((energies,)),
            pltpu.SemaphoreType.DMA((energies,)),
            pltpu.SemaphoreType.DMA((energies,)),
            pltpu.SemaphoreType.DMA((energies,)),
        ],
        compiler_params=pltpu.CompilerParams(
            collective_id=0, has_side_effects=True, vmem_limit_bytes=63 * 2**20
        ),
    )(
        propagator.reshape(2, orb, orb),
        forward_source.reshape(orb, cols),
        backward_source.reshape(orb, cols),
        left_orbital.reshape(pairs // LANES, LANES),
        right_orbital.reshape(pairs // LANES, LANES),
        phonon_shift,
        coupling,
    )
    return out.reshape(2, 1, pairs)


def solution(mesh):
    placed = (
        P("energy", "section", None, None, None),
        P("energy", "section", None, None),
        P("energy", "section", None, None),
        P("section"),
        P("section"),
        P(),
        P(None, "section"),
    )
    return jax.shard_map(
        on_device,
        mesh=mesh,
        in_specs=placed,
        out_specs=P(None, "energy", "section"),
        check_vma=False,
    )
```

```python
import functools
import jax
import jax.numpy as jnp
from jax import lax
from jax.experimental import pallas as pl
from jax.experimental.pallas import tpu as pltpu
from jax.sharding import PartitionSpec as P

MESH = pl.DeviceIdType.MESH
F32 = jnp.float32
BF16 = jnp.bfloat16
LANES = 128
DEEP = 256
DEEP_BITS = 8
FOLD = 64
REACH = 6


def partner(me, j, count):
    if count & (count - 1):
        return lax.rem(me + j, count)
    found, bit = 0, 1
    while bit < count:
        mine = lax.rem(me // bit, 2)
        asked = lax.rem(j // bit, 2)
        found = found + bit * (mine + asked - 2 * mine * asked)
        bit *= 2
    return found


def sweep_kernel(
    energies, sections,
    prop_hbm, fsrc_hbm, bsrc_hbm, left_hbm, right_hbm, shift_ref, coup_hbm,
    out_ref,
    prop, fsrc, bsrc, left, right, coup,
    bsrc_t, chosen, weight,
    y, w_t, y_in, w_in, w_end,
    table, parts, sent, held, totals, gathered,
    load_sems, fwd_send, fwd_recv, bwd_send, bwd_recv, end_send, end_recv,
    send_one, recv_one, send_two, recv_two,
):
    me = lax.axis_index("energy")
    s = lax.axis_index("section")
    orb = prop.shape[1]
    cols = y.shape[1]
    half = cols // 2
    block = chosen.shape[2]
    rows = block // LANES
    groups = table.shape[0] // (2 * FOLD)

    barrier = pltpu.get_barrier_semaphore()
    for j in range(1, energies):
        pl.semaphore_signal(
            barrier, inc=1, device_id={"energy": lax.rem(me + j, energies)}, device_id_type=MESH
        )

    @pl.when(s > 0)
    def _():
        pl.semaphore_signal(barrier, inc=1, device_id={"section": s - 1}, device_id_type=MESH)

    @pl.when(s < sections - 1)
    def _():
        pl.semaphore_signal(barrier, inc=1, device_id={"section": s + 1}, device_id_type=MESH)

    own = pl.ds(pl.multiple_of(me * block, LANES), block)
    loads = [
        pltpu.make_async_copy(fsrc_hbm, fsrc, load_sems.at[0]),
        pltpu.make_async_copy(bsrc_hbm, bsrc, load_sems.at[1]),
        pltpu.make_async_copy(left_hbm, left, load_sems.at[2]),
        pltpu.make_async_copy(right_hbm, right, load_sems.at[3]),
        pltpu.make_async_copy(prop_hbm, prop, load_sems.at[4]),
        pltpu.make_async_copy(coup_hbm.at[:, own], coup, load_sems.at[5]),
    ]
    for load in loads:
        load.start()

    table[...] = jnp.zeros(table.shape, table.dtype)
    zeros = jnp.zeros((REACH,) + held.shape[1:], held.dtype)
    held[pl.ds(0, REACH)] = zeros
    held[pl.ds(REACH + energies, REACH)] = zeros

    after, before = lax.rem(s + 1, sections), lax.rem(s + sections - 1, sections)

    def passed(source, target, send_sem, recv_sem, to):
        return pltpu.make_async_remote_copy(
            src_ref=source, dst_ref=target, send_sem=send_sem, recv_sem=recv_sem,
            device_id={"section": to}, device_id_type=MESH,
        )

    fwd_first = passed(fsrc_hbm, y_in, fwd_send, fwd_recv, after)
    fwd = passed(y, y_in, fwd_send, fwd_recv, after)
    bwd_first = passed(bsrc_hbm, w_end, end_send, end_recv, before)
    bwd = passed(w_t, w_in, bwd_send, bwd_recv, before)
    base = s * orb

    def choose(b, carry):
        spot = lax.broadcasted_iota(jnp.int32, (DEEP, LANES), 0)
        for i in range(rows):
            row = (left[pl.ds(b * rows + i, 1), :] - base) & (DEEP - 1)
            chosen[b, :, i * LANES:(i + 1) * LANES] = jnp.where(spot == row, 1.0, 0.0).astype(BF16)
        return carry

    greeted = (energies - 1) + (s > 0).astype(jnp.int32) + (s < sections - 1).astype(jnp.int32)
    pl.semaphore_wait(barrier, greeted)

    @pl.when(s == 0)
    def _():
        fwd_first.start()

    @pl.when(s == sections - 1)
    def _():
        bwd_first.start()

    for at in (0, 1, 2):
        loads[at].wait()
    bsrc_t[...] = bsrc[...].astype(F32).T

    @pl.when(s == 0)
    def _():
        y[...] = fsrc[...]

    @pl.when(s == sections - 1)
    def _():
        w_t[...] = bsrc_t[...].astype(BF16)

    def build(t):
        lax.fori_loop(
            t * energies // (sections - 1), (t + 1) * energies // (sections - 1), choose, 0
        )

    build(0)
    loads[4].wait()

    def turn(t, carry):
        @pl.when(s == t)
        def _():
            fwd.wait_recv()
            current = y_in[...]
            first = jnp.dot(prop[0], current, preferred_element_type=F32)
            second = jnp.dot(prop[1], current, preferred_element_type=F32)
            lane = lax.broadcasted_iota(jnp.int32, second.shape, 1)
            crossed = pltpu.roll(second, half, 1)
            crossed = jnp.where(lane < half, -crossed, crossed)
            y[...] = (first + crossed + fsrc[...].astype(F32)).astype(BF16)

            @pl.when(s < sections - 1)
            def _():
                fwd.start()

        @pl.when(s == sections - 1 - t)
        def _():
            @pl.when(t == 1)
            def _():
                bwd_first.wait_recv()
                w_in[...] = w_end[...].astype(F32).T.astype(BF16)

            @pl.when(t > 1)
            def _():
                bwd.wait_recv()

            current = w_in[...]
            first = jnp.dot(current, prop[0], preferred_element_type=F32)
            second = jnp.dot(current, prop[1], preferred_element_type=F32)
            crossed = jnp.concatenate([second[half:], -second[:half]], axis=0)
            w_t[...] = (first + crossed + bsrc_t[...]).astype(BF16)

            @pl.when(s > 0)
            def _():
                bwd.start()

        @pl.when(t < sections - 1)
        def _():
            build(t)

        return carry

    lax.fori_loop(1, sections, turn, 0)
    loads[3].wait()
    loads[5].wait()

    for k in range(coup.shape[0]):
        for i in range(rows):
            line = coup[k:k + 1, i * LANES:(i + 1) * LANES]
            weight[k, i:i + 1, :] = line
            weight[k, rows + i:rows + i + 1, :] = line

    scale = half ** (-0.5)
    ahead = y[...]
    wide = ahead.astype(F32)
    lane = lax.broadcasted_iota(jnp.int32, wide.shape, 1)
    turned = pltpu.roll(wide, half, 1)
    turned = jnp.where(lane < half, turned, -turned).astype(BF16)
    behind = w_t[...].astype(F32).T.astype(BF16)
    both = (((1,), (1,)), ((), ()))
    for member, operand in enumerate((ahead, turned)):
        product = lax.dot_general(behind, operand, both, preferred_element_type=F32)
        for tile in range(orb // LANES):
            folded = None
            for q in range(max(0, tile * 2 - 1), min(orb // FOLD, tile * 2 + 3)):
                piece = product[q * FOLD:(q + 1) * FOLD, tile * LANES:(tile + 1) * LANES]
                right_at = q * FOLD + lax.broadcasted_iota(jnp.int32, piece.shape, 0)
                left_at = tile * LANES + lax.broadcasted_iota(jnp.int32, piece.shape, 1)
                kept = jnp.where(jnp.abs(right_at - left_at) < FOLD // 2, piece, 0.0)
                folded = kept if folded is None else folded + kept
            group, column = tile * LANES // DEEP, tile * LANES % DEEP
            top = (member * groups + group) * FOLD
            table[top:top + FOLD, column:column + LANES] = (folded * scale).astype(BF16)

    def exchange_one(other):
        return pltpu.make_async_remote_copy(
            src_ref=sent.at[other], dst_ref=held.at[REACH + me],
            send_sem=send_one.at[other], recv_sem=recv_one.at[me],
            device_id={"energy": other}, device_id_type=MESH,
        )

    def exchange_two(other):
        return pltpu.make_async_remote_copy(
            src_ref=totals.at[other], dst_ref=gathered.at[me],
            send_sem=send_two.at[other], recv_sem=recv_two.at[me],
            device_id={"energy": other}, device_id_type=MESH,
        )

    def arrived(other, sems, buffer, at):
        return pltpu.make_async_remote_copy(
            src_ref=buffer.at[at], dst_ref=buffer.at[at],
            send_sem=sems.at[other], recv_sem=sems.at[other],
            device_id={"energy": other}, device_id_type=MESH,
        )

    def product_of(b):
        return jnp.dot(table[...], chosen[b], preferred_element_type=F32)

    def pick(b, spread):
        eight = (8, LANES)
        for i in range(rows):
            right_at = (right[pl.ds(b * rows + i, 1), :] - base) & (FOLD - 1)
            group = lax.shift_right_logical(left[pl.ds(b * rows + i, 1), :] - base, DEEP_BITS)
            high = jnp.broadcast_to(
                group * (FOLD // 8) + lax.shift_right_logical(right_at, 3), eight
            )
            low = lax.broadcasted_iota(jnp.int32, eight, 0) == jnp.broadcast_to(right_at & 7, eight)
            for member in range(2):
                top = member * groups * FOLD
                pieces = [
                    spread[top + 8 * n:top + 8 * n + 8, i * LANES:(i + 1) * LANES]
                    for n in range(groups * FOLD // 8)
                ]
                width = 1 << (len(pieces) - 1).bit_length()
                while width > 1:
                    width //= 2
                    upper = (high & width) != 0
                    pieces = [
                        jnp.where(upper, pieces[n + width], piece)
                        if n + width < len(pieces) else piece
                        for n, piece in enumerate(pieces[:width])
                    ]
                parts[b, pl.ds(member * rows + i, 1), :] = jnp.sum(
                    jnp.where(low, pieces[0], 0.0), axis=0, keepdims=True
                )
        return parts[b].astype(BF16)

    if energies <= 8:
        order = [partner(me, jnp.int32(j), energies) for j in range(energies - 1, 0, -1)]
        spread = product_of(order[0])
        for at, other in enumerate(order):
            current = spread
            spread = product_of(order[at + 1] if at + 1 < len(order) else me)
            sent[other] = pick(other, current)
            exchange_one(other).start()
        held[REACH + me] = pick(me, spread)
    else:
        def serve(j, carry):
            other = partner(me, energies - j, energies)
            sent[other] = pick(other, product_of(other))
            exchange_one(other).start()
            return carry

        lax.fori_loop(1, energies, serve, 0)
        held[REACH + me] = pick(me, product_of(me))

    def await_one(j, carry):
        other = partner(me, energies - j, energies)
        arrived(other, recv_one, held, REACH + other).wait_recv()
        return carry

    lax.fori_loop(1, energies, await_one, 0)

    total = None
    for k in range(coup.shape[0]):
        moved = held[pl.ds(REACH - shift_ref[k], energies)].astype(F32)
        term = weight[k][None] * moved
        total = term if total is None else total + term
    totals[...] = total.astype(BF16)

    def send_back(j, carry):
        exchange_two(partner(me, energies - j, energies)).start()
        return carry

    lax.fori_loop(1, energies, send_back, 0)
    gathered[me] = totals[me]

    def await_two(j, carry):
        other = partner(me, energies - j, energies)
        arrived(other, recv_two, gathered, other).wait_recv()
        return carry

    lax.fori_loop(1, energies, await_two, 0)
    for b in range(energies):
        for member in range(2):
            out_ref[member, b * rows:(b + 1) * rows, :] = gathered[
                b, member * rows:(member + 1) * rows, :
            ].astype(F32)

    def settle(j, carry):
        other = partner(me, energies - j, energies)
        exchange_one(other).wait_send()
        exchange_two(other).wait_send()
        return carry

    lax.fori_loop(1, energies, settle, 0)

    @pl.when(s < sections - 1)
    def _():
        fwd.wait_send()

    @pl.when(s == sections - 1)
    def _():
        bwd_first.wait_send()

    @pl.when((s > 0) & (s < sections - 1))
    def _():
        bwd.wait_send()


def on_device(
    propagator, forward_source, backward_source, left_orbital, right_orbital, phonon_shift, coupling
):
    energies = lax.axis_size("energy")
    sections = lax.axis_size("section")
    orb = propagator.shape[3]
    cols = forward_source.shape[3]
    pairs = left_orbital.shape[0]
    phonons = coupling.shape[0]
    block = pairs // energies
    rows = block // LANES
    tall = max(16, 2 * rows)
    groups = pl.cdiv(orb, DEEP)
    in_hbm = pl.BlockSpec(memory_space=pltpu.HBM)
    out = pl.pallas_call(
        functools.partial(sweep_kernel, energies, sections),
        out_shape=jax.ShapeDtypeStruct((2, pairs // LANES, LANES), F32),
        in_specs=[in_hbm] * 5 + [pl.BlockSpec(memory_space=pltpu.SMEM), in_hbm],
        out_specs=pl.BlockSpec(memory_space=pltpu.VMEM),
        scratch_shapes=[
            pltpu.VMEM((2, orb, orb), BF16),
            pltpu.VMEM((orb, cols), BF16),
            pltpu.VMEM((orb, cols), BF16),
            pltpu.VMEM((pairs // LANES, LANES), jnp.int32),
            pltpu.VMEM((pairs // LANES, LANES), jnp.int32),
            pltpu.VMEM((phonons, block), F32),
            pltpu.VMEM((cols, orb), F32),
            pltpu.VMEM((energies, DEEP, block), BF16),
            pltpu.VMEM((phonons, tall, LANES), F32),
            pltpu.VMEM((orb, cols), BF16),
            pltpu.VMEM((cols, orb), BF16),
            pltpu.VMEM((orb, cols), BF16),
            pltpu.VMEM((cols, orb), BF16),
            pltpu.VMEM((orb, cols), BF16),
            pltpu.VMEM((2 * groups * FOLD, DEEP), BF16),
            pltpu.VMEM((energies, tall, LANES), F32),
            pltpu.VMEM((energies, tall, LANES), BF16),
            pltpu.VMEM((energies + 2 * REACH, tall, LANES), BF16),
            pltpu.VMEM((energies, tall, LANES), BF16),
            pltpu.VMEM((energies, tall, LANES), BF16),
            pltpu.SemaphoreType.DMA((6,)),
            pltpu.SemaphoreType.DMA,
            pltpu.SemaphoreType.DMA,
            pltpu.SemaphoreType.DMA,
            pltpu.SemaphoreType.DMA,
            pltpu.SemaphoreType.DMA,
            pltpu.SemaphoreType.DMA,
            pltpu.SemaphoreType.DMA((energies,)),
            pltpu.SemaphoreType.DMA((energies,)),
            pltpu.SemaphoreType.DMA((energies,)),
            pltpu.SemaphoreType.DMA((energies,)),
        ],
        compiler_params=pltpu.CompilerParams(
            collective_id=0, has_side_effects=True, vmem_limit_bytes=63 * 2**20
        ),
    )(
        propagator.reshape(2, orb, orb),
        forward_source.reshape(orb, cols),
        backward_source.reshape(orb, cols),
        left_orbital.reshape(pairs // LANES, LANES),
        right_orbital.reshape(pairs // LANES, LANES),
        phonon_shift,
        coupling,
    )
    return out.reshape(2, 1, pairs)


def solution(mesh):
    placed = (
        P("energy", "section", None, None, None),
        P("energy", "section", None, None),
        P("energy", "section", None, None),
        P("section"),
        P("section"),
        P(),
        P(None, "section"),
    )
    return jax.shard_map(
        on_device,
        mesh=mesh,
        in_specs=placed,
        out_specs=P(None, "energy", "section"),
        check_vma=False,
    )
```

```python
import functools
import jax
import jax.numpy as jnp
from jax import lax
from jax.experimental import pallas as pl
from jax.experimental.pallas import tpu as pltpu
from jax.sharding import PartitionSpec as P

MESH = pl.DeviceIdType.MESH
F32 = jnp.float32
BF16 = jnp.bfloat16
LANES = 128
DEEP = 256
DEEP_BITS = 8
FOLD = 64
REACH = 6


def partner(me, j, count):
    if count & (count - 1):
        return lax.rem(me + j, count)
    found, bit = 0, 1
    while bit < count:
        mine = lax.rem(me // bit, 2)
        asked = lax.rem(j // bit, 2)
        found = found + bit * (mine + asked - 2 * mine * asked)
        bit *= 2
    return found


def sweep_kernel(
    energies, sections,
    prop_hbm, fsrc_hbm, bsrc_hbm, left_hbm, right_hbm, shift_ref, coup_hbm,
    out_ref,
    prop, fsrc, bsrc, left, right, coup,
    bsrc_t, chosen, weight,
    y, w_t, y_in, w_in, w_end,
    table, parts, sent, held, totals, gathered,
    load_sems, fwd_send, fwd_recv, bwd_send, bwd_recv, end_send, end_recv,
    send_one, recv_one, send_two, recv_two,
):
    me = lax.axis_index("energy")
    s = lax.axis_index("section")
    orb = prop.shape[1]
    cols = y.shape[1]
    half = cols // 2
    block = chosen.shape[2]
    rows = block // LANES
    groups = table.shape[0] // (2 * FOLD)

    barrier = pltpu.get_barrier_semaphore()
    for j in range(1, energies):
        pl.semaphore_signal(
            barrier, inc=1, device_id={"energy": lax.rem(me + j, energies)}, device_id_type=MESH
        )

    @pl.when(s > 0)
    def _():
        pl.semaphore_signal(barrier, inc=1, device_id={"section": s - 1}, device_id_type=MESH)

    @pl.when(s < sections - 1)
    def _():
        pl.semaphore_signal(barrier, inc=1, device_id={"section": s + 1}, device_id_type=MESH)

    own = pl.ds(pl.multiple_of(me * block, LANES), block)
    loads = [
        pltpu.make_async_copy(fsrc_hbm, fsrc, load_sems.at[0]),
        pltpu.make_async_copy(bsrc_hbm, bsrc, load_sems.at[1]),
        pltpu.make_async_copy(left_hbm, left, load_sems.at[2]),
        pltpu.make_async_copy(right_hbm, right, load_sems.at[3]),
        pltpu.make_async_copy(prop_hbm, prop, load_sems.at[4]),
        pltpu.make_async_copy(coup_hbm.at[:, own], coup, load_sems.at[5]),
    ]
    for load in loads:
        load.start()

    table[...] = jnp.zeros(table.shape, table.dtype)
    zeros = jnp.zeros((REACH,) + held.shape[1:], held.dtype)
    held[pl.ds(0, REACH)] = zeros
    held[pl.ds(REACH + energies, REACH)] = zeros

    after, before = lax.rem(s + 1, sections), lax.rem(s + sections - 1, sections)

    def passed(source, target, send_sem, recv_sem, to):
        return pltpu.make_async_remote_copy(
            src_ref=source, dst_ref=target, send_sem=send_sem, recv_sem=recv_sem,
            device_id={"section": to}, device_id_type=MESH,
        )

    cuts = ((0, DEEP), (DEEP, orb))
    fwd_first, fwd, bwd_first, bwd = [], [], [], []
    for n, (low, high) in enumerate(cuts):
        span = pl.ds(low, high - low)
        fwd_first.append(
            passed(fsrc_hbm.at[span], y_in.at[span], fwd_send.at[n], fwd_recv.at[n], after)
        )
        fwd.append(passed(y.at[span], y_in.at[span], fwd_send.at[n], fwd_recv.at[n], after))
        bwd_first.append(
            passed(bsrc_hbm.at[span], w_end.at[span], end_send.at[n], end_recv.at[n], before)
        )
        bwd.append(
            passed(w_t.at[:, span], w_in.at[:, span], bwd_send.at[n], bwd_recv.at[n], before)
        )

    base = s * orb

    def choose(b, carry):
        spot = lax.broadcasted_iota(jnp.int32, (DEEP, LANES), 0)
        for i in range(rows):
            row = (left[pl.ds(b * rows + i, 1), :] - base) & (DEEP - 1)
            chosen[b, :, i * LANES:(i + 1) * LANES] = jnp.where(spot == row, 1.0, 0.0).astype(BF16)
        return carry

    greeted = (energies - 1) + (s > 0).astype(jnp.int32) + (s < sections - 1).astype(jnp.int32)
    pl.semaphore_wait(barrier, greeted)

    @pl.when(s == 0)
    def _():
        for piece in fwd_first:
            piece.start()

    @pl.when(s == sections - 1)
    def _():
        for piece in bwd_first:
            piece.start()

    for at in (0, 1, 2):
        loads[at].wait()
    bsrc_t[...] = bsrc[...].astype(F32).T

    @pl.when(s == 0)
    def _():
        y[...] = fsrc[...]

    @pl.when(s == sections - 1)
    def _():
        w_t[...] = bsrc_t[...].astype(BF16)

    def build(t):
        lax.fori_loop(
            t * energies // (sections - 1), (t + 1) * energies // (sections - 1), choose, 0
        )

    build(0)
    loads[4].wait()

    def turn(t, carry):
        @pl.when(s == t)
        def _():
            sums = [None, None]
            for n, (low, high) in enumerate(cuts):
                fwd[n].wait_recv()
                current = y_in[low:high]
                if n == 0:
                    sums = [
                        jnp.dot(prop[c, :, low:high], current, preferred_element_type=F32)
                        for c in range(2)
                    ]
            lane = lax.broadcasted_iota(jnp.int32, (orb, cols), 1)
            for n, (top, end) in enumerate(cuts):
                first, second = [
                    sums[c][top:end] + jnp.dot(
                        prop[c, top:end, low:high], current, preferred_element_type=F32
                    )
                    for c in range(2)
                ]
                crossed = pltpu.roll(second, half, 1)
                crossed = jnp.where(lane[top:end] < half, -crossed, crossed)
                y[top:end] = (first + crossed + fsrc[top:end].astype(F32)).astype(BF16)

                @pl.when(s < sections - 1)
                def _(n=n):
                    fwd[n].start()

        @pl.when(s == sections - 1 - t)
        def _():
            sums = [None, None]
            for n, (low, high) in enumerate(cuts):
                @pl.when(t == 1)
                def _(n=n, low=low, high=high):
                    bwd_first[n].wait_recv()
                    w_in[:, low:high] = w_end[low:high].astype(F32).T.astype(BF16)

                @pl.when(t > 1)
                def _(n=n):
                    bwd[n].wait_recv()

                current = w_in[:, low:high]
                if n == 0:
                    sums = [
                        jnp.dot(current, prop[c, low:high, :], preferred_element_type=F32)
                        for c in range(2)
                    ]
            for n, (top, end) in enumerate(cuts):
                first, second = [
                    sums[c][:, top:end] + jnp.dot(
                        current, prop[c, low:high, top:end], preferred_element_type=F32
                    )
                    for c in range(2)
                ]
                crossed = jnp.concatenate([second[half:], -second[:half]], axis=0)
                w_t[:, top:end] = (first + crossed + bsrc_t[:, top:end]).astype(BF16)

                @pl.when(s > 0)
                def _(n=n):
                    bwd[n].start()

        @pl.when(t < sections - 1)
        def _():
            build(t)

        return carry

    lax.fori_loop(1, sections, turn, 0)
    loads[3].wait()
    loads[5].wait()

    for k in range(coup.shape[0]):
        for i in range(rows):
            line = coup[k:k + 1, i * LANES:(i + 1) * LANES]
            weight[k, i:i + 1, :] = line
            weight[k, rows + i:rows + i + 1, :] = line

    scale = half ** (-0.5)
    ahead = y[...]
    wide = ahead.astype(F32)
    lane = lax.broadcasted_iota(jnp.int32, wide.shape, 1)
    turned = pltpu.roll(wide, half, 1)
    turned = jnp.where(lane < half, turned, -turned).astype(BF16)
    behind = w_t[...].astype(F32).T.astype(BF16)
    both = (((1,), (1,)), ((), ()))
    for member, operand in enumerate((ahead, turned)):
        product = lax.dot_general(behind, operand, both, preferred_element_type=F32)
        for tile in range(orb // LANES):
            folded = None
            for q in range(max(0, tile * 2 - 1), min(orb // FOLD, tile * 2 + 3)):
                piece = product[q * FOLD:(q + 1) * FOLD, tile * LANES:(tile + 1) * LANES]
                right_at = q * FOLD + lax.broadcasted_iota(jnp.int32, piece.shape, 0)
                left_at = tile * LANES + lax.broadcasted_iota(jnp.int32, piece.shape, 1)
                kept = jnp.where(jnp.abs(right_at - left_at) < FOLD // 2, piece, 0.0)
                folded = kept if folded is None else folded + kept
            group, column = tile * LANES // DEEP, tile * LANES % DEEP
            top = (member * groups + group) * FOLD
            table[top:top + FOLD, column:column + LANES] = (folded * scale).astype(BF16)

    def exchange_one(other):
        return pltpu.make_async_remote_copy(
            src_ref=sent.at[other], dst_ref=held.at[REACH + me],
            send_sem=send_one.at[other], recv_sem=recv_one.at[me],
            device_id={"energy": other}, device_id_type=MESH,
        )

    def exchange_two(other):
        return pltpu.make_async_remote_copy(
            src_ref=totals.at[other], dst_ref=gathered.at[me],
            send_sem=send_two.at[other], recv_sem=recv_two.at[me],
            device_id={"energy": other}, device_id_type=MESH,
        )

    def arrived(other, sems, buffer, at):
        return pltpu.make_async_remote_copy(
            src_ref=buffer.at[at], dst_ref=buffer.at[at],
            send_sem=sems.at[other], recv_sem=sems.at[other],
            device_id={"energy": other}, device_id_type=MESH,
        )

    def product_of(b):
        return jnp.dot(table[...], chosen[b], preferred_element_type=F32)

    def pick(b, spread):
        eight = (8, LANES)
        for i in range(rows):
            right_at = (right[pl.ds(b * rows + i, 1), :] - base) & (FOLD - 1)
            group = lax.shift_right_logical(left[pl.ds(b * rows + i, 1), :] - base, DEEP_BITS)
            high = jnp.broadcast_to(
                group * (FOLD // 8) + lax.shift_right_logical(right_at, 3), eight
            )
            low = lax.broadcasted_iota(jnp.int32, eight, 0) == jnp.broadcast_to(right_at & 7, eight)
            for member in range(2):
                top = member * groups * FOLD
                pieces = [
                    spread[top + 8 * n:top + 8 * n + 8, i * LANES:(i + 1) * LANES]
                    for n in range(groups * FOLD // 8)
                ]
                width = 1 << (len(pieces) - 1).bit_length()
                while width > 1:
                    width //= 2
                    upper = (high & width) != 0
                    pieces = [
                        jnp.where(upper, pieces[n + width], piece)
                        if n + width < len(pieces) else piece
                        for n, piece in enumerate(pieces[:width])
                    ]
                parts[b, pl.ds(member * rows + i, 1), :] = jnp.sum(
                    jnp.where(low, pieces[0], 0.0), axis=0, keepdims=True
                )
        return parts[b].astype(BF16)

    if energies <= 8:
        order = [partner(me, jnp.int32(j), energies) for j in range(energies - 1, 0, -1)]
        spread = product_of(order[0])
        for at, other in enumerate(order):
            current = spread
            spread = product_of(order[at + 1] if at + 1 < len(order) else me)
            sent[other] = pick(other, current)
            exchange_one(other).start()
        held[REACH + me] = pick(me, spread)
    else:
        def serve(j, carry):
            other = partner(me, energies - j, energies)
            sent[other] = pick(other, product_of(other))
            exchange_one(other).start()
            return carry

        lax.fori_loop(1, energies, serve, 0)
        held[REACH + me] = pick(me, product_of(me))

    def await_one(j, carry):
        other = partner(me, energies - j, energies)
        arrived(other, recv_one, held, REACH + other).wait_recv()
        return carry

    lax.fori_loop(1, energies, await_one, 0)

    total = None
    for k in range(coup.shape[0]):
        moved = held[pl.ds(REACH - shift_ref[k], energies)].astype(F32)
        term = weight[k][None] * moved
        total = term if total is None else total + term
    totals[...] = total.astype(BF16)

    def send_back(j, carry):
        exchange_two(partner(me, energies - j, energies)).start()
        return carry

    lax.fori_loop(1, energies, send_back, 0)
    gathered[me] = totals[me]

    def await_two(j, carry):
        other = partner(me, energies - j, energies)
        arrived(other, recv_two, gathered, other).wait_recv()
        return carry

    lax.fori_loop(1, energies, await_two, 0)
    for b in range(energies):
        for member in range(2):
            out_ref[member, b * rows:(b + 1) * rows, :] = gathered[
                b, member * rows:(member + 1) * rows, :
            ].astype(F32)

    def settle(j, carry):
        other = partner(me, energies - j, energies)
        exchange_one(other).wait_send()
        exchange_two(other).wait_send()
        return carry

    lax.fori_loop(1, energies, settle, 0)

    @pl.when(s < sections - 1)
    def _():
        for piece in fwd:
            piece.wait_send()

    @pl.when(s == sections - 1)
    def _():
        for piece in bwd_first:
            piece.wait_send()

    @pl.when((s > 0) & (s < sections - 1))
    def _():
        for piece in bwd:
            piece.wait_send()


def on_device(
    propagator, forward_source, backward_source, left_orbital, right_orbital, phonon_shift, coupling
):
    energies = lax.axis_size("energy")
    sections = lax.axis_size("section")
    orb = propagator.shape[3]
    cols = forward_source.shape[3]
    pairs = left_orbital.shape[0]
    phonons = coupling.shape[0]
    block = pairs // energies
    rows = block // LANES
    tall = max(16, 2 * rows)
    groups = pl.cdiv(orb, DEEP)
    in_hbm = pl.BlockSpec(memory_space=pltpu.HBM)
    out = pl.pallas_call(
        functools.partial(sweep_kernel, energies, sections),
        out_shape=jax.ShapeDtypeStruct((2, pairs // LANES, LANES), F32),
        in_specs=[in_hbm] * 5 + [pl.BlockSpec(memory_space=pltpu.SMEM), in_hbm],
        out_specs=pl.BlockSpec(memory_space=pltpu.VMEM),
        scratch_shapes=[
            pltpu.VMEM((2, orb, orb), BF16),
            pltpu.VMEM((orb, cols), BF16),
            pltpu.VMEM((orb, cols), BF16),
            pltpu.VMEM((pairs // LANES, LANES), jnp.int32),
            pltpu.VMEM((pairs // LANES, LANES), jnp.int32),
            pltpu.VMEM((phonons, block), F32),
            pltpu.VMEM((cols, orb), F32),
            pltpu.VMEM((energies, DEEP, block), BF16),
            pltpu.VMEM((phonons, tall, LANES), F32),
            pltpu.VMEM((orb, cols), BF16),
            pltpu.VMEM((cols, orb), BF16),
            pltpu.VMEM((orb, cols), BF16),
            pltpu.VMEM((cols, orb), BF16),
            pltpu.VMEM((orb, cols), BF16),
            pltpu.VMEM((2 * groups * FOLD, DEEP), BF16),
            pltpu.VMEM((energies, tall, LANES), F32),
            pltpu.VMEM((energies, tall, LANES), BF16),
            pltpu.VMEM((energies + 2 * REACH, tall, LANES), BF16),
            pltpu.VMEM((energies, tall, LANES), BF16),
            pltpu.VMEM((energies, tall, LANES), BF16),
            pltpu.SemaphoreType.DMA((6,)),
            pltpu.SemaphoreType.DMA((2,)),
            pltpu.SemaphoreType.DMA((2,)),
            pltpu.SemaphoreType.DMA((2,)),
            pltpu.SemaphoreType.DMA((2,)),
            pltpu.SemaphoreType.DMA((2,)),
            pltpu.SemaphoreType.DMA((2,)),
            pltpu.SemaphoreType.DMA((energies,)),
            pltpu.SemaphoreType.DMA((energies,)),
            pltpu.SemaphoreType.DMA((energies,)),
            pltpu.SemaphoreType.DMA((energies,)),
        ],
        compiler_params=pltpu.CompilerParams(
            collective_id=0, has_side_effects=True, vmem_limit_bytes=63 * 2**20
        ),
    )(
        propagator.reshape(2, orb, orb),
        forward_source.reshape(orb, cols),
        backward_source.reshape(orb, cols),
        left_orbital.reshape(pairs // LANES, LANES),
        right_orbital.reshape(pairs // LANES, LANES),
        phonon_shift,
        coupling,
    )
    return out.reshape(2, 1, pairs)


def solution(mesh):
    placed = (
        P("energy", "section", None, None, None),
        P("energy", "section", None, None),
        P("energy", "section", None, None),
        P("section"),
        P("section"),
        P(),
        P(None, "section"),
    )
    return jax.shard_map(
        on_device,
        mesh=mesh,
        in_specs=placed,
        out_specs=P(None, "energy", "section"),
        check_vma=False,
    )
```
